32 devices in a mesh: mp: 2 (over x), row: 16 (over z, y, core).
Axes of the slice: x: 2, y: 2, z: 4, core: 2. Of those that a mesh axis runs over, the one named last changes fastest.
Arguments:
- radial_funcs: bfloat16 [128, 1024], P('row'), may hold values from -6 to 6
- kernels: bfloat16 [80, 1024], P('mp'), parts along dimension 0, may hold values from -0.0010299683 to 0.0010299683
- wigner: float32 [40, 128], replicated, may hold values from -4 to 4
- sources: bfloat16 [64, 2048], P('mp', 'row'), parts along dimension 0, may hold values from -6 to 6
- wigner_slots: int32 [2048], P('row'), may hold values from 0 to 127
- owners: int32 [2048], P('row'), may hold values from 0 to 7, as said below
- degrees: int32 [128], P('row'), may hold values from 0 to 30
- frequencies: float32 [2048], P('row'), may hold values from 0.5 to 2
Outputs:
- response: float32 [64, 2048], P('mp', 'row'), parts along dimension 0
The draws below stay inside these ranges and needn't reach their ends.
There are 2 independent parts, one for each index of `mp`. The reference program is written for one: setup_inputs(seed, part) draws one part's arguments, and reference() takes and returns one part's arrays. A program takes and returns all parts, laid end to end along the dimension named above; an argument that names none is the same for every part. Nothing has to cross between parts.
Inputs may be any that keep to these rules, and one draw needn't show every extreme that they name: Within each aligned block of 128 singlets, owners never falls and every value 0 to 7 occurs.
All inputs are finite; a program needn't handle non-finite values.
Results may differ from the reference program's by a relative error of at most 0.0055.
Values may be sent and summed in bfloat16 or wider, within the bound.
A program may use at most 128 MiB of HBM per device.

```python
import jax
import jax.numpy as jnp
from jax import lax

R = 1024
S = 40
NSRC = 32
WQ = 128
LMAX = 30
SD = 128
MD = 8
M = 128
NS = 2048
N_ROW = 16


def draw_owners(key, part):
    keys = jax.random.split(jax.random.fold_in(key, 7), N_ROW)

    def one_block(block_key):
        shuffled = jax.random.permutation(block_key, SD - 1) + 1
        cuts = jnp.sort(shuffled[:MD - 1])
        places = jnp.arange(SD, dtype=jnp.int32)
        return jnp.sum((cuts[None, :] <= places[:, None]).astype(jnp.int32), axis=1).astype(jnp.int32)
    return jax.vmap(one_block)(keys).reshape(-1).astype(jnp.int32)


def with_ends(array, own_key, smallest, largest):
    shape = array.shape
    spot = [jax.random.randint(jax.random.fold_in(own_key, axis), (), 0, shape[axis]) for axis in range(len(shape))]
    array = array.at[tuple(spot)].set(smallest)
    longest = shape.index(max(shape))
    spot[longest] = (spot[longest] + 1) % shape[longest]
    return array.at[tuple(spot)].set(largest)


def levels(stream_key, shape, cuts, low, high):
    gain, own = 1.0, jax.random.fold_in(stream_key, 6)
    for axis_at, blocks in cuts:
        draws = jnp.exp(jax.random.uniform(jax.random.fold_in(own, axis_at), (blocks,), jnp.float32, low / len(cuts), high / len(cuts)))
        gain = gain * jnp.repeat(draws, shape[axis_at] // blocks).reshape([-1 if axis == axis_at else 1 for axis in range(len(shape))])
    return gain


def scatter_about(key, dims, scale, limit, cuts=(), kind=jnp.bfloat16):
    drawn = jax.random.normal(key, dims, jnp.float32) * scale
    if len(cuts) > 0:
        drawn = levels(key, dims, cuts, -0.22, 0.18) * drawn
    return jnp.clip(drawn, min=-limit, max=limit).astype(kind)


def setup_inputs(seed: int = 0, part: int = 0) -> dict:
    streams_of = jax.random.split(jax.random.key(seed), 9)
    own_keys = jax.random.split(jax.random.fold_in(streams_of[8], part), 9)
    radial_funcs = scatter_about(streams_of[0], (M, R), 1.0, 6.0, ((0, 16),))
    kernels = scatter_about(own_keys[1], (S, R), ((0.4 * S * M * R * SD / MD) ** -0.5), 0.0010299683)
    wigner = scatter_about(streams_of[2], (S, WQ), 1.0, 4.0, (), jnp.float32)
    sources = scatter_about(own_keys[3], (NSRC, NS), 1.0, 6.0, ((1, 16),))
    wigner_slots = with_ends(jax.random.randint(streams_of[4], (NS,), 0, WQ), jax.random.fold_in(streams_of[4], 1), 0, WQ - 1).astype(jnp.int32)
    owners = draw_owners(jax.random.fold_in(streams_of[8], 71), part)
    degrees = with_ends(jax.random.randint(streams_of[6], (M,), 0, LMAX + 1), jax.random.fold_in(streams_of[6], 1), 0, LMAX).astype(jnp.int32)
    frequencies = jnp.clip(0.5 + 1.5 * jax.random.uniform(streams_of[7], (NS,), jnp.float32) ** levels(streams_of[7], (NS,), ((0, 16),), -0.2, 0.2), 0.5, 2.0)
    return dict(radial_funcs=radial_funcs, kernels=kernels, wigner=wigner, sources=sources, wigner_slots=wigner_slots, owners=owners, degrees=degrees, frequencies=frequencies)


def lookup(wigner, slot_block):
    return jnp.take(wigner, slot_block, axis=1)


def project(source_block, slot_block, owner_block, wigner, mult_dev):
    angular = lookup(wigner, slot_block)
    member = (owner_block[:, None] == jnp.arange(mult_dev, dtype=jnp.int32)[None, :]).astype(jnp.float32)
    scaled = angular[:, None, :] * source_block.astype(jnp.float32)[None, :, :]
    return jnp.einsum('skj,ja->ska', scaled, member, precision=lax.Precision.HIGHEST)


def selection(near_deg, far_deg, num_degree):
    level = jnp.arange(num_degree, dtype=jnp.int32)[:, None, None]
    total_deg = near_deg[None, :, None] + far_deg[None, None, :]
    diff_deg = jnp.abs(near_deg[None, :, None] - far_deg[None, None, :])
    return (diff_deg <= level) & (level <= total_deg) & ((total_deg + level) % 2 == 0)


def reference(radial_funcs, kernels, wigner, sources, wigner_slots, owners, degrees, frequencies):
    src_blocks = sources.reshape(NSRC, N_ROW, SD).transpose(1, 0, 2)
    slot_blocks = wigner_slots.reshape(N_ROW, SD)
    owner_blocks = owners.reshape(N_ROW, SD)
    freq_blocks = frequencies.reshape(N_ROW, SD)
    eig_blocks = radial_funcs.reshape(N_ROW, MD, R)
    deg_blocks = degrees.reshape(N_ROW, MD)
    built = jax.vmap(lambda src_one, slot_one, owner_one: project(src_one, slot_one, owner_one, wigner, MD))(
        src_blocks, slot_blocks, owner_blocks)
    projected = built.transpose(1, 2, 0, 3).reshape(S, NSRC, M).astype(jnp.bfloat16)

    def row_block(inputs):
        eig_one, deg_one, src_one, slot_one, owner_one, freq_one = inputs
        weighted = (eig_one.astype(jnp.float32)[None] * kernels.astype(jnp.float32)[:, None, :]).astype(jnp.bfloat16)
        integral = lax.dot_general(weighted.reshape(S * MD, R), radial_funcs, (((1,), (1,)), ((), ())),
                                   preferred_element_type=jnp.float32).reshape(S, MD, M)
        integral = jnp.where(selection(deg_one, degrees, S), integral, jnp.float32(0.0)).astype(jnp.bfloat16)
        coupled = jnp.einsum('sab,skb->ska', integral.astype(jnp.float32), projected.astype(jnp.float32))
        angular = lookup(wigner, slot_one)
        member = (owner_one[None, :] == jnp.arange(MD, dtype=jnp.int32)[:, None]).astype(jnp.float32)
        spread = jnp.einsum('ska,ai->ski', coupled, member, precision=lax.Precision.HIGHEST)
        return freq_one[None, :] * src_one.astype(jnp.float32) + jnp.sum(angular[:, None, :] * spread, axis=0)

    result = lax.map(row_block, (eig_blocks, deg_blocks, src_blocks, slot_blocks, owner_blocks, freq_blocks))
    return result.transpose(1, 0, 2).reshape(NSRC, NS)
```

```python
import functools

import jax
import jax.numpy as jnp
from jax import lax
from jax.experimental import pallas as pl
from jax.experimental.pallas import tpu as pltpu
from jax.sharding import PartitionSpec as P

MESH = pl.DeviceIdType.MESH
BF16 = jnp.bfloat16
F32 = jnp.float32
I32 = jnp.int32
LANES = 128


def grid_of(n):
    chips = n // 2
    inner = max(d for d in range(1, chips + 1) if chips % d == 0 and d * d <= chips)
    return chips // inner, inner


def halves(value):
    high = value.astype(BF16)
    return high, (value - high.astype(F32)).astype(BF16)


def kernel(
    n, rad_ref, ker_ref, wig_ref, src_ref, slot_ref, own_ref, deg_ref, freq_ref,
    out_ref, fbuf, pbuf, send_sem, recv_sem,
):
    outer, inner = grid_of(n)
    me = lax.axis_index("row")
    core = lax.rem(me, 2)
    chip = lax.div(me, 2)
    my_in = lax.rem(chip, inner)
    my_out = lax.div(chip, inner)

    def index(o, i, c):
        return (o * inner + i) * 2 + c

    def at_out(step):
        return lax.rem(my_out + step, outer)

    def at_in(step):
        return lax.rem(my_in + step, inner)

    out_peers = [index(at_out(t), my_in, core) for t in range(1, outer)]
    in_peers = [index(my_out, at_in(t), core) for t in range(1, inner)]
    sibling = index(my_out, my_in, 1 - core)
    peers = out_peers + in_peers + [sibling]

    barrier = pltpu.get_barrier_semaphore()
    for peer in peers:
        pl.semaphore_signal(barrier, inc=1, device_id={"row": peer}, device_id_type=MESH)

    bufs = (fbuf, pbuf)
    started = []
    counts = [0, 0]

    def send(part, slot, peer):
        copy = pltpu.make_async_remote_copy(
            src_ref=bufs[part].at[slot],
            dst_ref=bufs[part].at[slot],
            send_sem=send_sem.at[part, counts[part]],
            recv_sem=recv_sem.at[part, slot],
            device_id={"row": peer},
            device_id_type=MESH,
        )
        counts[part] += 1
        copy.start()
        started.append(copy)

    def arrived(part, slot):
        pltpu.make_async_remote_copy(
            src_ref=bufs[part].at[slot],
            dst_ref=bufs[part].at[slot],
            send_sem=send_sem.at[part, 0],
            recv_sem=recv_sem.at[part, slot],
            device_id={"row": sibling},
            device_id_type=MESH,
        ).wait_recv()

    def send_own(part):
        for peer in out_peers + in_peers + [sibling]:
            send(part, me, peer)

    def pass_out(part):
        for slot in out_peers:
            arrived(part, slot)
            for peer in in_peers + [sibling]:
                send(part, slot, peer)

    def pass_in(part):
        for o in range(outer):
            for i in range(1, inner):
                slot = index(at_out(o), at_in(i), core)
                arrived(part, slot)
                send(part, slot, sibling)

    def last(part):
        for o in range(outer):
            for i in range(inner):
                arrived(part, index(at_out(o), at_in(i), 1 - core))

    mult, nodes = rad_ref.shape
    num_degree, table = wig_ref.shape
    nsrc, width = src_ref.shape
    half_nodes = nodes // 2
    half_deg = num_degree // 2
    half_lanes = half_deg * nsrc

    rad = rad_ref[...].astype(F32)
    deg_row = deg_ref[...].astype(F32)
    eye = lax.broadcasted_iota(I32, (mult, mult), 0) == lax.broadcasted_iota(I32, (mult, mult), 1)
    deg_col = jnp.sum(jnp.where(eye, deg_row, 0.0), axis=1, keepdims=True)
    deg_block = jnp.broadcast_to(deg_col, (mult, LANES))
    fbuf[me, :, :half_nodes] = jnp.concatenate(
        [rad[:, :half_nodes], rad[:, half_nodes:]], axis=0
    ).astype(BF16)
    fbuf[me, :, half_nodes:] = jnp.concatenate([deg_block, deg_block], axis=0).astype(BF16)
    pl.semaphore_wait(barrier, len(peers))
    send_own(0)

    hot = (lax.broadcasted_iota(I32, (table, width), 0) == slot_ref[...]).astype(F32).astype(BF16)
    wig_high, wig_low = halves(wig_ref[...])
    angular = jnp.dot(wig_high, hot, preferred_element_type=F32) + jnp.dot(
        wig_low, hot, preferred_element_type=F32
    )
    member = (lax.broadcasted_iota(I32, (mult, width), 0) == own_ref[...]).astype(F32)
    src = src_ref[...].astype(F32)
    scaled = (angular[:, None, :] * src[None, :, :]).reshape(num_degree * nsrc, width)
    scaled_high, scaled_low = halves(scaled)
    member16 = member.astype(BF16)
    dims = (((1,), (1,)), ((), ()))
    own_part = lax.dot_general(
        jnp.concatenate([member16, member16], axis=1),
        jnp.concatenate([scaled_high, scaled_low], axis=1),
        dims,
        preferred_element_type=F32,
    )
    pbuf[me] = jnp.concatenate(
        [own_part[:, :half_lanes], own_part[:, half_lanes:]], axis=0
    ).astype(BF16)
    send_own(1)

    pass_out(0)

    ker = ker_ref[...].astype(F32)
    weighted = (ker[:, None, :] * rad[None, :, :]).reshape(num_degree * mult, nodes).astype(BF16)
    placed = (angular[:, None, :] * member[None, :, :]).reshape(num_degree * mult, width)
    placed_high, placed_low = halves(placed)

    pass_in(0)
    pass_out(1)
    last(0)

    far = n * 2 * mult
    funcs = fbuf[...].reshape(far, half_nodes + LANES)
    ones = jnp.full((mult, LANES), 1.0 / LANES, BF16)
    far_deg = lax.dot_general(
        ones, funcs[:, half_nodes:], dims, preferred_element_type=F32
    ).astype(I32)
    near_deg = deg_col.astype(I32)
    total = near_deg + far_deg
    apart = jnp.abs(near_deg - far_deg)
    odd = total & 1
    second = (lax.broadcasted_iota(I32, (mult, far), 1) & mult) // mult
    never = jnp.int32(1 << 20)
    least = [
        [jnp.where((odd == p) & (second == h), apart, never) for p in range(2)] for h in range(2)
    ]
    top = lax.dot_general(
        weighted[:, :half_nodes], funcs[:, :half_nodes], dims, preferred_element_type=F32
    )
    low = lax.dot_general(
        weighted[:, half_nodes:], funcs[:, :half_nodes], dims, preferred_element_type=F32
    )
    edge = half_deg * mult
    first_sum = top[:edge] + pltpu.roll(low[:edge], far - mult, axis=1)
    second_sum = low[edge:] + pltpu.roll(top[edge:], mult, axis=1)
    rows = []
    for s in range(num_degree):
        h = s // half_deg
        value = (first_sum, second_sum)[h][(s - h * half_deg) * mult:(s - h * half_deg + 1) * mult]
        keep = (least[h][s % 2] <= s) & (total >= s)
        rows.append(jnp.where(keep, value, 0.0))

    pass_in(1)
    last(1)

    per = LANES // nsrc
    lane_of = lax.broadcasted_iota(I32, (per * mult, LANES), 1) // nsrc
    row_of = lax.broadcasted_iota(I32, (per * mult, LANES), 0) // mult
    diagonal = lane_of == row_of
    pieces = [[], []]
    for g in range(half_lanes // LANES):
        lhs = jnp.concatenate(
            [rows[h * half_deg + g * per + t] for h in range(2) for t in range(per)], axis=0
        ).astype(BF16)
        rhs = pbuf[:, :, g * LANES:(g + 1) * LANES].reshape(far, LANES)
        both = jnp.dot(lhs, rhs, preferred_element_type=F32)
        for h in range(2):
            pieces[h].append(jnp.where(diagonal, both[h * per * mult:(h + 1) * per * mult], 0.0))
    coupled = jnp.concatenate(pieces[0] + pieces[1], axis=0)
    coupled_high, coupled_low = halves(coupled)
    spread = lax.dot_general(
        jnp.concatenate([coupled_high, coupled_low, coupled_high], axis=0),
        jnp.concatenate([placed_high, placed_high, placed_low], axis=0),
        (((0,), (0,)), ((), ())),
        preferred_element_type=F32,
    )
    result = freq_ref[...] * src
    for t in range(per):
        result = result + spread[t * nsrc:(t + 1) * nsrc]
    out_ref[...] = result
    for copy in started:
        copy.wait_send()


def local(n, radial_funcs, kernels, wigner, sources, wigner_slots, owners, degrees, frequencies):
    mult, nodes = radial_funcs.shape
    num_degree = kernels.shape[0]
    nsrc, width = sources.shape
    return pl.pallas_call(
        functools.partial(kernel, n),
        out_shape=jax.ShapeDtypeStruct((nsrc, width), F32),
        in_specs=[pl.BlockSpec(memory_space=pltpu.VMEM)] * 8,
        out_specs=pl.BlockSpec(memory_space=pltpu.VMEM),
        scratch_shapes=[
            pltpu.VMEM((n, 2 * mult, nodes // 2 + LANES), BF16),
            pltpu.VMEM((n, 2 * mult, num_degree * nsrc // 2), BF16),
            pltpu.SemaphoreType.DMA((2, n - 1)),
            pltpu.SemaphoreType.DMA((2, n)),
        ],
        compiler_params=pltpu.CompilerParams(
            collective_id=0, has_side_effects=True, vmem_limit_bytes=(8 << 20) + n * (256 << 10)
        ),
    )(
        radial_funcs, kernels, wigner, sources, wigner_slots.reshape(1, -1), owners.reshape(1, -1),
        degrees.reshape(1, -1), frequencies.reshape(1, -1),
    )


def solution(mesh):
    in_specs = (
        P("row", None),
        P("mp", None),
        P(),
        P("mp", "row"),
        P("row"),
        P("row"),
        P("row"),
        P("row"),
    )
    out_specs = P("mp", "row")
    return jax.shard_map(
        functools.partial(local, mesh.shape["row"]),
        mesh=mesh,
        in_specs=in_specs,
        out_specs=out_specs,
        check_vma=False,
    )
```

```python
import functools

import jax
import jax.numpy as jnp
from jax import lax
from jax.experimental import pallas as pl
from jax.experimental.pallas import tpu as pltpu
from jax.sharding import PartitionSpec as P

MESH = pl.DeviceIdType.MESH
BF16 = jnp.bfloat16
F32 = jnp.float32
I32 = jnp.int32
LANES = 128
ROOM = 60 << 20


def grid_of(n):
    chips = n // 2
    inner = max(d for d in range(1, chips + 1) if chips % d == 0 and d * d <= chips)
    return chips // inner, inner


def halves(value):
    high = value.astype(BF16)
    return high, (value - high.astype(F32)).astype(BF16)


def kernel(
    n, rad_hbm, ker_hbm, wig_hbm, src_hbm, slot_hbm, own_hbm, deg_hbm, freq_hbm, out_ref,
    rad_ref, ker_ref, wig_ref, src_ref, slot_ref, own_ref, deg_ref, freq_ref,
    fbuf, pbuf, load_sem, send_sem, recv_sem,
):
    outer, inner = grid_of(n)
    me = lax.axis_index("row")
    core = lax.rem(me, 2)
    chip = lax.div(me, 2)
    my_in = lax.rem(chip, inner)
    my_out = lax.div(chip, inner)

    def index(o, i, c):
        return (o * inner + i) * 2 + c

    def at_out(step):
        return lax.rem(my_out + step, outer)

    def at_in(step):
        return lax.rem(my_in + step, inner)

    outs = [at_out(t) for t in range(1, outer)]
    ins = [at_in(t) for t in range(1, inner)]
    other = 1 - core
    every = slice(None)
    sibling = index(my_out, my_in, other)
    out_peers = [index(o, my_in, core) for o in outs]
    in_peers = [index(my_out, i, core) for i in ins]
    peers = out_peers + in_peers + [sibling]

    barrier = pltpu.get_barrier_semaphore()
    for peer in peers:
        pl.semaphore_signal(barrier, inc=1, device_id={"row": peer}, device_id_type=MESH)

    sources = (rad_hbm, deg_hbm, wig_hbm, slot_hbm, own_hbm, src_hbm, ker_hbm, freq_hbm)
    held = (rad_ref, deg_ref, wig_ref, slot_ref, own_ref, src_ref, ker_ref, freq_ref)
    loads = [
        pltpu.make_async_copy(here, there, load_sem.at[k])
        for k, (here, there) in enumerate(zip(sources, held))
    ]
    for load in loads:
        load.start()

    bufs = (fbuf, pbuf)
    started = []
    counts = [0, 0]

    def describe(part, view, key, peer):
        return pltpu.make_async_remote_copy(
            src_ref=bufs[part].at[view],
            dst_ref=bufs[part].at[view],
            send_sem=send_sem.at[part, counts[part]],
            recv_sem=recv_sem.at[part, key],
            device_id={"row": peer},
            device_id_type=MESH,
        )

    def send(part, view, key, peer):
        copy = describe(part, view, key, peer)
        counts[part] += 1
        copy.start()
        started.append(copy)

    def arrived(part, view, key):
        describe(part, view, key, sibling).wait_recv()

    mine = (my_out, my_in, core)

    mult, nodes = rad_ref.shape
    num_degree, table = wig_ref.shape
    nsrc, width = src_ref.shape
    half_nodes = nodes // 2
    half_deg = num_degree // 2
    half_lanes = half_deg * nsrc

    for load in loads[:2]:
        load.wait()
    rad = rad_ref[...].astype(F32)
    deg_row = deg_ref[...].astype(F32)
    eye = lax.broadcasted_iota(I32, (mult, mult), 0) == lax.broadcasted_iota(I32, (mult, mult), 1)
    deg_col = jnp.sum(jnp.where(eye, deg_row, 0.0), axis=1, keepdims=True)
    deg_block = jnp.broadcast_to(deg_col, (mult, LANES))
    fbuf[my_out, my_in, core, :, :half_nodes] = jnp.concatenate(
        [rad[:, :half_nodes], rad[:, half_nodes:]], axis=0
    ).astype(BF16)
    fbuf[my_out, my_in, core, :, half_nodes:] = jnp.concatenate([deg_block, deg_block], axis=0).astype(BF16)
    pl.semaphore_wait(barrier, len(peers))
    for peer in in_peers:
        send(0, mine, me, peer)

    for load in loads[2:6]:
        load.wait()
    hot = (lax.broadcasted_iota(I32, (table, width), 0) == slot_ref[...]).astype(F32).astype(BF16)
    wig_high, wig_low = halves(wig_ref[...])
    angular = jnp.dot(wig_high, hot, preferred_element_type=F32) + jnp.dot(
        wig_low, hot, preferred_element_type=F32
    )
    member = (lax.broadcasted_iota(I32, (mult, width), 0) == own_ref[...]).astype(F32)
    src = src_ref[...].astype(F32)
    scaled = (angular[:, None, :] * src[None, :, :]).reshape(num_degree * nsrc, width)
    scaled_high, scaled_low = halves(scaled)
    member16 = member.astype(BF16)
    dims = (((1,), (1,)), ((), ()))
    own_part = lax.dot_general(
        jnp.concatenate([member16, member16], axis=1),
        jnp.concatenate([scaled_high, scaled_low], axis=1),
        dims,
        preferred_element_type=F32,
    )
    pbuf[my_out, my_in, core] = jnp.concatenate(
        [own_part[:, :half_lanes], own_part[:, half_lanes:]], axis=0
    ).astype(BF16)
    for peer in out_peers:
        send(1, mine, me, peer)

    for load in loads[6:]:
        load.wait()
    ker = ker_ref[...].astype(F32)
    weighted = (ker[:, None, :] * rad[None, :, :]).reshape(num_degree * mult, nodes).astype(BF16)
    placed = (angular[:, None, :] * member[None, :, :]).reshape(num_degree * mult, width)
    placed_high, placed_low = halves(placed)

    for i in ins:
        arrived(0, (my_out, i, core), index(my_out, i, core))
    for peer in out_peers:
        send(0, (my_out, every, core), n + my_out, peer)
    send(0, (my_out, every, core), n + outer + my_out, sibling)
    for o in outs:
        arrived(1, (o, my_in, core), index(o, my_in, core))
    for peer in in_peers:
        send(1, (every, my_in, core), n + my_in, peer)
    send(1, (every, my_in, core), n + inner + my_in, sibling)
    for o in outs:
        arrived(0, (o, every, core), n + o)
        send(0, (o, every, core), n + outer + o, sibling)
    for i in ins:
        arrived(1, (every, i, core), n + i)
        send(1, (every, i, core), n + inner + i, sibling)
    for o in [my_out] + outs:
        arrived(0, (o, every, other), n + outer + o)

    far = n * 2 * mult
    funcs = fbuf[...].reshape(far, half_nodes + LANES)
    ones = jnp.full((mult, LANES), 1.0 / LANES, BF16)
    far_deg = lax.dot_general(
        ones, funcs[:, half_nodes:], dims, preferred_element_type=F32
    ).astype(I32)
    near_deg = deg_col.astype(I32)
    total = near_deg + far_deg
    apart = jnp.abs(near_deg - far_deg)
    odd = total & 1
    second = (lax.broadcasted_iota(I32, (mult, far), 1) & mult) // mult
    never = jnp.int32(1 << 20)
    least = [
        [jnp.where((odd == p) & (second == h), apart, never) for p in range(2)] for h in range(2)
    ]
    top = lax.dot_general(
        weighted[:, :half_nodes], funcs[:, :half_nodes], dims, preferred_element_type=F32
    )
    low = lax.dot_general(
        weighted[:, half_nodes:], funcs[:, :half_nodes], dims, preferred_element_type=F32
    )
    edge = half_deg * mult
    first_sum = top[:edge] + pltpu.roll(low[:edge], far - mult, axis=1)
    second_sum = low[edge:] + pltpu.roll(top[edge:], mult, axis=1)
    rows = []
    for s in range(num_degree):
        h = s // half_deg
        value = (first_sum, second_sum)[h][(s - h * half_deg) * mult:(s - h * half_deg + 1) * mult]
        keep = (least[h][s % 2] <= s) & (total >= s)
        rows.append(jnp.where(keep, value, 0.0))

    for i in [my_in] + ins:
        arrived(1, (every, i, other), n + inner + i)

    per = LANES // nsrc
    lane_of = lax.broadcasted_iota(I32, (per * mult, LANES), 1) // nsrc
    row_of = lax.broadcasted_iota(I32, (per * mult, LANES), 0) // mult
    diagonal = lane_of == row_of
    pieces = [[], []]
    for g in range(half_lanes // LANES):
        lhs = jnp.concatenate(
            [rows[h * half_deg + g * per + t] for h in range(2) for t in range(per)], axis=0
        ).astype(BF16)
        rhs = pbuf[..., g * LANES:(g + 1) * LANES].reshape(far, LANES)
        both = jnp.dot(lhs, rhs, preferred_element_type=F32)
        for h in range(2):
            pieces[h].append(jnp.where(diagonal, both[h * per * mult:(h + 1) * per * mult], 0.0))
    coupled = jnp.concatenate(pieces[0] + pieces[1], axis=0)
    coupled_high, coupled_low = halves(coupled)
    spread = lax.dot_general(
        jnp.concatenate([coupled_high, coupled_low, coupled_high], axis=0),
        jnp.concatenate([placed_high, placed_high, placed_low], axis=0),
        (((0,), (0,)), ((), ())),
        preferred_element_type=F32,
    )
    result = freq_ref[...] * src
    for t in range(per):
        result = result + spread[t * nsrc:(t + 1) * nsrc]
    out_ref[...] = result
    for copy in started:
        copy.wait_send()


def local(n, radial_funcs, kernels, wigner, sources, wigner_slots, owners, degrees, frequencies):
    mult, nodes = radial_funcs.shape
    num_degree = kernels.shape[0]
    nsrc, width = sources.shape
    outer, inner = grid_of(n)
    arrays = (
        radial_funcs, kernels, wigner, sources, wigner_slots.reshape(1, -1), owners.reshape(1, -1),
        degrees.reshape(1, -1), frequencies.reshape(1, -1),
    )
    return pl.pallas_call(
        functools.partial(kernel, n),
        out_shape=jax.ShapeDtypeStruct((nsrc, width), F32),
        in_specs=[pl.BlockSpec(memory_space=pltpu.HBM)] * len(arrays),
        out_specs=pl.BlockSpec(memory_space=pltpu.VMEM),
        scratch_shapes=[pltpu.VMEM(a.shape, a.dtype) for a in arrays] + [
            pltpu.VMEM((outer, inner, 2, 2 * mult, nodes // 2 + LANES), BF16),
            pltpu.VMEM((outer, inner, 2, 2 * mult, num_degree * nsrc // 2), BF16),
            pltpu.SemaphoreType.DMA((len(arrays),)),
            pltpu.SemaphoreType.DMA((2, 2 * (outer + inner))),
            pltpu.SemaphoreType.DMA((2, n + 2 * max(outer, inner))),
        ],
        compiler_params=pltpu.CompilerParams(
            collective_id=0, has_side_effects=True, vmem_limit_bytes=ROOM
        ),
    )(*arrays)


def solution(mesh):
    in_specs = (
        P("row", None),
        P("mp", None),
        P(),
        P("mp", "row"),
        P("row"),
        P("row"),
        P("row"),
        P("row"),
    )
    out_specs = P("mp", "row")
    return jax.shard_map(
        functools.partial(local, mesh.shape["row"]),
        mesh=mesh,
        in_specs=in_specs,
        out_specs=out_specs,
        check_vma=False,
    )
```

```python
import functools

import jax
import jax.numpy as jnp
from jax import lax
from jax.experimental import pallas as pl
from jax.experimental.pallas import tpu as pltpu
from jax.sharding import PartitionSpec as P

MESH = pl.DeviceIdType.MESH
BF16 = jnp.bfloat16
F32 = jnp.float32
I32 = jnp.int32
LANES = 128


def grid_of(n):
    chips = n // 2
    inner = max(d for d in range(1, chips + 1) if chips % d == 0 and d * d <= chips)
    return chips // inner, inner


def halves(value):
    high = value.astype(BF16)
    return high, (value - high.astype(F32)).astype(BF16)


def kernel(
    n, rad_hbm, ker_hbm, wig_hbm, src_hbm, slot_hbm, own_hbm, deg_hbm, freq_hbm, out_ref,
    rad_ref, ker_ref, wig_ref, src_ref, slot_ref, own_ref, deg_ref, freq_ref,
    fbuf, pbuf, load_sem, send_sem, recv_sem,
):
    outer, inner = grid_of(n)
    me = lax.axis_index("row")
    core = lax.rem(me, 2)
    chip = lax.div(me, 2)
    my_in = lax.rem(chip, inner)
    my_out = lax.div(chip, inner)

    def index(o, i, c):
        return (o * inner + i) * 2 + c

    def at_out(step):
        return lax.rem(my_out + step, outer)

    def at_in(step):
        return lax.rem(my_in + step, inner)

    outs = [at_out(t) for t in range(1, outer)]
    ins = [at_in(t) for t in range(1, inner)]
    other = 1 - core
    every = slice(None)
    sibling = index(my_out, my_in, other)
    out_peers = [index(o, my_in, core) for o in outs]
    in_peers = [index(my_out, i, core) for i in ins]
    peers = out_peers + in_peers + [sibling]

    barrier = pltpu.get_barrier_semaphore()
    for peer in peers:
        pl.semaphore_signal(barrier, inc=1, device_id={"row": peer}, device_id_type=MESH)

    sources = (rad_hbm, deg_hbm, wig_hbm, slot_hbm, own_hbm, src_hbm, ker_hbm, freq_hbm)
    held = (rad_ref, deg_ref, wig_ref, slot_ref, own_ref, src_ref, ker_ref, freq_ref)
    loads = [
        pltpu.make_async_copy(here, there, load_sem.at[k])
        for k, (here, there) in enumerate(zip(sources, held))
    ]
    for load in loads:
        load.start()

    bufs = (fbuf, pbuf)
    started = []
    counts = [0, 0]

    def describe(part, view, key, peer):
        return pltpu.make_async_remote_copy(
            src_ref=bufs[part].at[view],
            dst_ref=bufs[part].at[view],
            send_sem=send_sem.at[part, counts[part]],
            recv_sem=recv_sem.at[part, key],
            device_id={"row": peer},
            device_id_type=MESH,
        )

    def send(part, view, key, peer):
        copy = describe(part, view, key, peer)
        counts[part] += 1
        copy.start()
        started.append(copy)

    def arrived(part, view, key):
        describe(part, view, key, sibling).wait_recv()

    mine = (my_out, my_in, core)

    mult, nodes = rad_ref.shape
    num_degree, table = wig_ref.shape
    nsrc, width = src_ref.shape
    half_nodes = nodes // 2
    half_deg = num_degree // 2
    half_lanes = half_deg * nsrc

    for load in loads[:2]:
        load.wait()
    rad = rad_ref[...].astype(F32)
    deg_row = deg_ref[...].astype(F32)
    eye = lax.broadcasted_iota(I32, (mult, mult), 0) == lax.broadcasted_iota(I32, (mult, mult), 1)
    deg_col = jnp.sum(jnp.where(eye, deg_row, 0.0), axis=1, keepdims=True)
    deg_block = jnp.broadcast_to(deg_col, (mult, LANES))
    fbuf[my_out, my_in, core, :, :half_nodes] = jnp.concatenate(
        [rad[:, :half_nodes], rad[:, half_nodes:]], axis=0
    ).astype(BF16)
    fbuf[my_out, my_in, core, :, half_nodes:] = jnp.concatenate([deg_block, deg_block], axis=0).astype(BF16)

    for load in loads[2:6]:
        load.wait()
    hot = (lax.broadcasted_iota(I32, (table, width), 0) == slot_ref[...]).astype(F32).astype(BF16)
    wig_high, wig_low = halves(wig_ref[...])
    angular = jnp.dot(wig_high, hot, preferred_element_type=F32) + jnp.dot(
        wig_low, hot, preferred_element_type=F32
    )
    member = (lax.broadcasted_iota(I32, (mult, width), 0) == own_ref[...]).astype(F32)
    src = src_ref[...].astype(F32)
    scaled = (angular[:, None, :] * src[None, :, :]).reshape(num_degree * nsrc, width)
    scaled_high, scaled_low = halves(scaled)
    member16 = member.astype(BF16)
    dims = (((1,), (1,)), ((), ()))
    own_part = lax.dot_general(
        jnp.concatenate([member16, member16], axis=1),
        jnp.concatenate([scaled_high, scaled_low], axis=1),
        dims,
        preferred_element_type=F32,
    )
    pbuf[my_out, my_in, core] = jnp.concatenate(
        [own_part[:, :half_lanes], own_part[:, half_lanes:]], axis=0
    ).astype(BF16)
    pl.semaphore_wait(barrier, len(peers))
    for peer in in_peers:
        send(0, mine, me, peer)
    for peer in out_peers:
        send(1, mine, me, peer)

    for load in loads[6:]:
        load.wait()
    ker = ker_ref[...].astype(F32)
    weighted = (ker[:, None, :] * rad[None, :, :]).reshape(num_degree * mult, nodes).astype(BF16)
    placed = (angular[:, None, :] * member[None, :, :]).reshape(num_degree * mult, width)
    placed_high, placed_low = halves(placed)

    for i in ins:
        arrived(0, (my_out, i, core), index(my_out, i, core))
    for peer in out_peers:
        send(0, (my_out, every, core), n + my_out, peer)
    send(0, (my_out, every, core), n + outer + my_out, sibling)
    for o in outs:
        arrived(1, (o, my_in, core), index(o, my_in, core))
    for peer in in_peers:
        send(1, (every, my_in, core), n + my_in, peer)
    send(1, (every, my_in, core), n + inner + my_in, sibling)
    for o in outs:
        arrived(0, (o, every, core), n + o)
        send(0, (o, every, core), n + outer + o, sibling)
    for i in ins:
        arrived(1, (every, i, core), n + i)
        send(1, (every, i, core), n + inner + i, sibling)
    for o in [my_out] + outs:
        arrived(0, (o, every, other), n + outer + o)

    far = n * 2 * mult
    funcs = fbuf[...].reshape(far, half_nodes + LANES)
    ones = jnp.full((mult, LANES), 1.0 / LANES, BF16)
    far_deg = lax.dot_general(
        ones, funcs[:, half_nodes:], dims, preferred_element_type=F32
    ).astype(I32)
    near_deg = deg_col.astype(I32)
    total = near_deg + far_deg
    apart = jnp.abs(near_deg - far_deg)
    odd = total & 1
    second = (lax.broadcasted_iota(I32, (mult, far), 1) & mult) // mult
    never = jnp.int32(1 << 20)
    least = [
        [jnp.where((odd == p) & (second == h), apart, never) for p in range(2)] for h in range(2)
    ]
    top = lax.dot_general(
        weighted[:, :half_nodes], funcs[:, :half_nodes], dims, preferred_element_type=F32
    )
    low = lax.dot_general(
        weighted[:, half_nodes:], funcs[:, :half_nodes], dims, preferred_element_type=F32
    )
    edge = half_deg * mult
    first_sum = top[:edge] + pltpu.roll(low[:edge], far - mult, axis=1)
    second_sum = low[edge:] + pltpu.roll(top[edge:], mult, axis=1)
    rows = []
    for s in range(num_degree):
        h = s // half_deg
        value = (first_sum, second_sum)[h][(s - h * half_deg) * mult:(s - h * half_deg + 1) * mult]
        keep = (least[h][s % 2] <= s) & (total >= s)
        rows.append(jnp.where(keep, value, 0.0))

    for i in [my_in] + ins:
        arrived(1, (every, i, other), n + inner + i)

    per = LANES // nsrc
    lane_of = lax.broadcasted_iota(I32, (per * mult, LANES), 1) // nsrc
    row_of = lax.broadcasted_iota(I32, (per * mult, LANES), 0) // mult
    diagonal = lane_of == row_of
    pieces = [[], []]
    for g in range(half_lanes // LANES):
        lhs = jnp.concatenate(
            [rows[h * half_deg + g * per + t] for h in range(2) for t in range(per)], axis=0
        ).astype(BF16)
        rhs = pbuf[..., g * LANES:(g + 1) * LANES].reshape(far, LANES)
        both = jnp.dot(lhs, rhs, preferred_element_type=F32)
        for h in range(2):
            pieces[h].append(jnp.where(diagonal, both[h * per * mult:(h + 1) * per * mult], 0.0))
    coupled = jnp.concatenate(pieces[0] + pieces[1], axis=0)
    coupled_high, coupled_low = halves(coupled)
    spread = lax.dot_general(
        jnp.concatenate([coupled_high, coupled_low, coupled_high], axis=0),
        jnp.concatenate([placed_high, placed_high, placed_low], axis=0),
        (((0,), (0,)), ((), ())),
        preferred_element_type=F32,
    )
    result = freq_ref[...] * src
    for t in range(per):
        result = result + spread[t * nsrc:(t + 1) * nsrc]
    out_ref[...] = result
    for copy in started:
        copy.wait_send()


def local(n, radial_funcs, kernels, wigner, sources, wigner_slots, owners, degrees, frequencies):
    mult, nodes = radial_funcs.shape
    num_degree = kernels.shape[0]
    nsrc, width = sources.shape
    outer, inner = grid_of(n)
    arrays = (
        radial_funcs, kernels, wigner, sources, wigner_slots.reshape(1, -1), owners.reshape(1, -1),
        degrees.reshape(1, -1), frequencies.reshape(1, -1),
    )
    return pl.pallas_call(
        functools.partial(kernel, n),
        out_shape=jax.ShapeDtypeStruct((nsrc, width), F32),
        in_specs=[pl.BlockSpec(memory_space=pltpu.HBM)] * len(arrays),
        out_specs=pl.BlockSpec(memory_space=pltpu.VMEM),
        scratch_shapes=[pltpu.VMEM(a.shape, a.dtype) for a in arrays] + [
            pltpu.VMEM((outer, inner, 2, 2 * mult, nodes // 2 + LANES), BF16),
            pltpu.VMEM((outer, inner, 2, 2 * mult, num_degree * nsrc // 2), BF16),
            pltpu.SemaphoreType.DMA((len(arrays),)),
            pltpu.SemaphoreType.DMA((2, 2 * (outer + inner))),
            pltpu.SemaphoreType.DMA((2, n + 2 * max(outer, inner))),
        ],
        compiler_params=pltpu.CompilerParams(
            collective_id=0, has_side_effects=True, vmem_limit_bytes=(8 << 20) + n * (256 << 10)
        ),
    )(*[pltpu.with_memory_space_constraint(a, pltpu.HBM) for a in arrays])


def solution(mesh):
    in_specs = (
        P("row", None),
        P("mp", None),
        P(),
        P("mp", "row"),
        P("row"),
        P("row"),
        P("row"),
        P("row"),
    )
    out_specs = P("mp", "row")
    return jax.shard_map(
        functools.partial(local, mesh.shape["row"]),
        mesh=mesh,
        in_specs=in_specs,
        out_specs=out_specs,
        check_vma=False,
    )
```
